512 devices in a mesh: layer: 2 (over x_hi), gx: 32 (over z, x_lo, core), gy: 8 (over y).
Axes of the slice: x: 4 (x_hi: 2, x_lo: 2; x = x_hi * 2 + x_lo), y: 8, z: 8, core: 2. Of those that a mesh axis runs over, the one named last changes fastest.
Arguments:
- prev_vec: float32 [2, 64, 32, 32, 128], P('layer', 'gx', 'gy'), may hold values from -6 to 6
- cur_vec: float32 [2, 64, 32, 32, 128], P('layer', 'gx', 'gy'), may hold values from -6 to 6
- displace: float32 [2, 64, 32, 2, 128], P('layer', 'gx', 'gy'), may hold values from -0.15 to 0.15
- potential: float32 [2, 64, 32, 128], P('layer', 'gx', 'gy'), may hold values from -1.5 to 1.5
Outputs:
- first_term: float32 [2, 64, 32, 32, 128], P('layer', 'gx', 'gy')
- second_term: float32 [2, 64, 32, 32, 128], P('layer', 'gx', 'gy')
The draws below stay inside these ranges and needn't reach their ends.
All inputs are finite; a program needn't handle non-finite values.
Results may differ from the reference program's by a relative error of at most 0.0003.
Values sent between devices are 32-bit elements; how exact they have to be, the bound alone decides.
A program may use at most 64 MiB of HBM per device.

```python
import math
import jax
import jax.numpy as jnp
from jax import lax

ORB = 128
VECS = 32
PATCH_X = 14
PATCH_Y = 4
NBX = 64
NBY = 32


def shard_levels(key, dims, cuts, least, top_value):
    gain, own = 1.0, jax.random.fold_in(key, 6)
    for dim, blocks in cuts:
        steps = jnp.exp(jax.random.uniform(jax.random.fold_in(own, dim), (blocks,), jnp.float32, least / len(cuts), top_value / len(cuts)))
        gain = gain * jnp.repeat(steps, dims[dim] // blocks).reshape([-1 if axis == dim else 1 for axis in range(len(dims))])
    return gain


def bell_draw(stream_key, shape, width, reach, cuts=(), kind=jnp.bfloat16):
    loudness = shard_levels(stream_key, shape, cuts, -0.22, 0.18) if cuts else 1.0
    entries = jax.random.normal(stream_key, shape, jnp.float32) * width * loudness
    return jnp.minimum(jnp.maximum(entries, -reach), reach).astype(kind)


def setup_inputs(seed: int = 0) -> dict:
    key_of = jax.random.split(jax.random.key(seed), 5)
    prev_vec = bell_draw(key_of[0], (2, NBX, NBY, VECS, ORB), 1.0, 6.0, ((0, 2), (1, 32), (2, 8)), jnp.float32)
    cur_vec = bell_draw(key_of[1], (2, NBX, NBY, VECS, ORB), 1.0, 6.0, ((0, 2), (1, 32), (2, 8)), jnp.float32)
    displace = jnp.clip(jax.random.uniform(key_of[2], (2, NBX, NBY, 2, ORB), jnp.float32, -0.15, 0.15) * shard_levels(key_of[2], (2, NBX, NBY, 2, ORB), ((0, 2), (1, 32), (2, 8)), -0.4, 0.0), -0.15, 0.15)
    potential = jnp.clip(jax.random.uniform(key_of[3], (2, NBX, NBY, ORB), jnp.float32, -1.5, 1.5) * shard_levels(key_of[3], (2, NBX, NBY, ORB), ((0, 2), (1, 32), (2, 8)), -0.4, 0.0), -1.5, 1.5)
    return {"prev_vec": prev_vec, "cur_vec": cur_vec, "displace": displace, "potential": potential}


v_pi = -2.7
v_sigma = 0.48
decay_len = 0.319
layer_gap = 3.35 / 1.42
cut_radius = 3.5
hop_scale = 12.0
twist_angle = 1.05 * math.pi / 180.0
root_three = math.sqrt(3.0)
cell_w = 4.0 * root_three
cell_h = 24.0

def lattice(cos_vals, sin_vals):
    orbital = jnp.arange(128, dtype=jnp.int32)
    sublattice = orbital % 4
    unit_cell = orbital // 4
    column_at = (unit_cell // 8).astype(jnp.float32)
    row_at = (unit_cell % 8).astype(jnp.float32)
    inner_x = jnp.where((sublattice == 1) | (sublattice == 2), root_three / 2.0, 0.0)
    inner_y = jnp.where(sublattice == 1, 0.5, jnp.where(sublattice == 2, 1.5, jnp.where(sublattice == 3, 2.0, 0.0)))
    pos_x = column_at * root_three + inner_x - cell_w / 2.0
    pos_y = row_at * 3.0 + inner_y - cell_h / 2.0
    rot_x = cos_vals[:, None] * pos_x - sin_vals[:, None] * pos_y
    rot_y = sin_vals[:, None] * pos_x + cos_vals[:, None] * pos_y
    return jnp.stack([rot_x, rot_y], axis=1).astype(jnp.float32)

def twist_offsets(cos_vals, sin_vals, row_ids, col_ids):
    along_x = cell_w * ((row_ids % PATCH_X).astype(jnp.float32) - (PATCH_X - 1) / 2.0)
    along_y = cell_h * ((col_ids % PATCH_Y).astype(jnp.float32) - (PATCH_Y - 1) / 2.0)
    cos_less = (cos_vals - 1.0)[:, None, None]
    sin_cast = sin_vals[:, None, None]
    shift_x = cos_less * along_x[None, :, None] - sin_cast * along_y[None, None, :]
    shift_y = sin_cast * along_x[None, :, None] + cos_less * along_y[None, None, :]
    return jnp.stack([shift_x, shift_y], axis=-1)[..., None]

def taper(dist_sq):
    scaled = dist_sq / (cut_radius * cut_radius)
    return jnp.maximum(1.0 - scaled * scaled, 0.0)

def plane_block(own_pos, near_pos, shift_x, shift_y, diagonal_zero):
    delta_x = own_pos[..., 0, :, None] - near_pos[..., 0, None, :] - shift_x
    delta_y = own_pos[..., 1, :, None] - near_pos[..., 1, None, :] - shift_y
    dist_sq = delta_x * delta_x + delta_y * delta_y
    spread = jnp.sqrt(dist_sq)
    hopping = v_pi * jnp.exp(-(spread - 1.0) / decay_len) * taper(dist_sq)
    if diagonal_zero:
        orbital = jnp.arange(128, dtype=jnp.int32)
        hopping = jnp.where(orbital[:, None] == orbital[None, :], 0.0, hopping)
    return hopping

def inter_block(own_pos, near_pos, shift_x, shift_y):
    delta_x = own_pos[..., 0, :, None] - near_pos[..., 0, None, :] - shift_x
    delta_y = own_pos[..., 1, :, None] - near_pos[..., 1, None, :] - shift_y
    dist_sq = delta_x * delta_x + delta_y * delta_y + layer_gap * layer_gap
    spread = jnp.sqrt(dist_sq)
    cosine_sq = layer_gap * layer_gap / dist_sq
    bonds = v_pi * jnp.exp(-(spread - 1.0) / decay_len) * (1.0 - cosine_sq) + v_sigma * jnp.exp(-(spread - layer_gap) / decay_len) * cosine_sq
    return bonds * taper(dist_sq)

def reference(prev_vec, cur_vec, displace, potential):
    cos_vals = jnp.array([1.0, math.cos(twist_angle)], dtype=jnp.float32)
    sin_vals = jnp.array([0.0, math.sin(twist_angle)], dtype=jnp.float32)
    places = displace + lattice(cos_vals, sin_vals)[:, None, None]
    row_count = places.shape[1]
    col_count = places.shape[2]
    twisted = places + twist_offsets(cos_vals, sin_vals, jnp.arange(row_count, dtype=jnp.int32), jnp.arange(col_count, dtype=jnp.int32))

    def apply_layer(vectors, layer_id):
        other_layer = 1 - layer_id
        cos_l = math.cos(twist_angle * layer_id)
        sin_l = math.sin(twist_angle * layer_id)

        def row_terms(row_id):
            own_pos = places[layer_id, row_id]
            own_twist = twisted[layer_id, row_id]
            summed = jnp.zeros((col_count, vectors.shape[3], 128), jnp.float32)
            for step_x in (-1, 0, 1):
                near_row = (row_id + step_x) % row_count
                row_pos = places[layer_id, near_row]
                row_vec = vectors[layer_id, near_row]
                far_pos = twisted[other_layer, near_row]
                far_vec = vectors[other_layer, near_row]
                for step_y in (-1, 0, 1):
                    near_pos = jnp.roll(row_pos, -step_y, axis=0)
                    near_vec = jnp.roll(row_vec, -step_y, axis=0)
                    shift_x = cos_l * step_x * cell_w - sin_l * step_y * cell_h
                    shift_y = sin_l * step_x * cell_w + cos_l * step_y * cell_h
                    hop_block = plane_block(own_pos, near_pos, shift_x, shift_y, step_x == 0 and step_y == 0)
                    summed = summed + jnp.einsum('ycq,ypq->ycp', near_vec, hop_block, precision=lax.Precision.HIGHEST)
                    cross_block = inter_block(own_twist, jnp.roll(far_pos, -step_y, axis=0), step_x * cell_w, step_y * cell_h)
                    summed = summed + jnp.einsum('ycq,ypq->ycp', jnp.roll(far_vec, -step_y, axis=0), cross_block, precision=lax.Precision.HIGHEST)
            summed = summed + potential[layer_id, row_id][:, None, :] * vectors[layer_id, row_id]
            return summed / hop_scale
        return lax.map(row_terms, jnp.arange(row_count, dtype=jnp.int32))

    def apply_hops(vectors):
        return jnp.stack([apply_layer(vectors, 0), apply_layer(vectors, 1)])
    first_term = 2.0 * apply_hops(cur_vec) - prev_vec
    second_term = 2.0 * apply_hops(first_term) - cur_vec
    return (first_term, second_term)
```

```python
import math

import jax
import jax.numpy as jnp
import numpy as np
from jax import lax
from jax.experimental import pallas as pl
from jax.experimental.pallas import tpu as pltpu
from jax.sharding import PartitionSpec as P

MESH = pl.DeviceIdType.MESH
PATCH_X = 14
PATCH_Y = 4

v_pi = -2.7
v_sigma = 0.48
decay_len = 0.319
layer_gap = 3.35 / 1.42
cut_radius = 3.5
hop_scale = 12.0
twist_angle = 1.05 * math.pi / 180.0
root_three = math.sqrt(3.0)
cell_w = 4.0 * root_three
cell_h = 24.0
reach = 0.15

COLS = 8
RIM = 2
WIDE = COLS + 2 * RIM
STEPS = 5
ROWS = 32
AUX = 8
FULL = ROWS + AUX
atom_x = (0.0, root_three / 2.0, root_three / 2.0, 0.0)
atom_y = (0.0, 0.5, 1.5, 2.0)


def near_offsets():
    cos_t, sin_t = math.cos(twist_angle), math.sin(twist_angle)
    cells = []
    for s in range(4):
        col, row = np.meshgrid(np.arange(4 * PATCH_X), np.arange(8 * PATCH_Y), indexing="ij")
        x = (col - 2 * PATCH_X) * root_three + atom_x[s]
        y = (row - 4 * PATCH_Y) * 3.0 + atom_y[s]
        cells.append(np.stack([x.ravel(), y.ravel()], -1))
    places = np.concatenate(cells)
    turn = np.array([[cos_t - 1.0, -sin_t], [sin_t, cos_t - 1.0]])
    drift = places @ turn.T
    drift = np.concatenate([drift, -drift])
    slack = 2.0 * reach + 1e-3
    flat = math.sqrt(cut_radius**2 - layer_gap**2)
    plane, inter = [], []
    for step in range(-STEPS - 2, STEPS + 3):
        for col in range(-RIM - 2, RIM + 3):
            hit_plane = hit_inter = False
            for s in range(4):
                t = (s + step) % 4
                x = atom_x[s] - atom_x[t] - col * root_three
                y = atom_y[s] - atom_y[t] - 3.0 * ((s + step) // 4)
                hit_plane |= math.hypot(x, y) - slack * math.sqrt(2.0) < cut_radius
                gap = np.maximum(np.abs(np.array([x, y]) + drift) - slack, 0.0)
                hit_inter |= bool((np.hypot(gap[:, 0], gap[:, 1]) < flat).any())
            if hit_plane and (col, step) != (0, 0):
                plane.append((col, step))
            if hit_inter:
                inter.append((col, step))
    assert max(abs(c) for c, _ in plane + inter) <= RIM
    assert max(abs(s) for _, s in plane + inter) <= STEPS
    return plane, inter


PLANE, INTER = near_offsets()
TILE = (1, 0, 0)
SIDES = [(a, b, 0) for a in (0, 1) for b in (-1, 1)]
ENDS = [(a, b, c) for a in (0, 1) for b in (-1, 0, 1) for c in (-1, 1)]
PEERS = SIDES + [TILE] + ENDS


def peer(step):
    sizes = [lax.axis_size(a) for a in ("layer", "gx", "gy")]
    return tuple(
        lax.rem(lax.axis_index(a) + s + n, n) for a, s, n in zip(("layer", "gx", "gy"), step, sizes)
    )


def pick(index, table):
    value = jnp.full(index.shape, table[3], jnp.float32)
    for s in range(3):
        value = jnp.where(index == s, jnp.float32(table[s]), value)
    return value


def regroup(parts, lane):
    group = lane // 32
    results = []
    for a in range(4):
        value = parts[a]
        for b in range(4):
            if b != a:
                value = jnp.where(group == b, pltpu.roll(parts[b], (32 * (b - a)) % 128, 1), value)
        results.append(value)
    return results


def kernel(
    prev_hbm, cur_hbm, disp_hbm, pot_hbm, first_ref, second_ref,
    prev_in, cur_in, disp_in, pot_in, aux, prev_t, wide, wide2, end_out, end_in, end_out2, end_in2,
    rolled, spot, spot_rim, near_plane, near_inter, hop_plane, hop_inter,
    load_sem, send_sem, recv_sem,
):
    barrier = pltpu.get_barrier_semaphore()
    for step in PEERS:
        pl.semaphore_signal(barrier, inc=1, device_id=peer(step), device_id_type=MESH)
    loads = [
        pltpu.make_async_copy(src, dst, load_sem.at[i])
        for i, (src, dst) in enumerate(
            ((cur_hbm, cur_in), (disp_hbm, disp_in), (pot_hbm, pot_in), (prev_hbm, prev_in))
        )
    ]
    for load in loads:
        load.start()
    lane = lax.broadcasted_iota(jnp.int32, (8, 128), 1)
    zero = jnp.zeros((8, 128), jnp.float32)

    def to_columns(source, target, rows, first):
        for x in range(2):
            for g in range(rows // 8):
                parts = [source[0, x, y, 8 * g : 8 * g + 8, :] for y in range(4)]
                for i, value in enumerate(regroup(parts, lane)):
                    target[first + 4 * x + i, 8 * g : 8 * g + 8, :] = value

    loads[0].wait()
    to_columns(cur_in, wide.at[0], ROWS, RIM)
    loads[1].wait()
    loads[2].wait()
    for x in range(2):
        for y in range(4):
            aux[x, y] = zero
            aux[x, y, 0:2] = disp_in[0, x, y]
            aux[x, y, 2:3] = pot_in[0, x, y : y + 1]
        for i, value in enumerate(regroup([aux[x, y] for y in range(4)], lane)):
            wide[0, RIM + 4 * x + i, ROWS:FULL, :] = value

    def pack_ends(source, target, aux_too):
        for part in range(2 if aux_too else 1):
            count = 32 if part == 0 else COLS
            low, high = zero, zero
            for k in range(count):
                col, row = (k // 4, 8 * (k % 4)) if part == 0 else (k, ROWS)
                value = pltpu.roll(source[0, RIM + col, row : row + 8, :], (4 * k + 4) % 128, 1)
                low = jnp.where(lane // 4 == k, value, low)
                high = jnp.where(lane // 4 == (k + 1) % 32, value, high)
            target[0, 8 * part : 8 * part + 8, :] = low
            target[1, 8 * part : 8 * part + 8, :] = high

    pack_ends(wide, end_out, True)

    def exchange(phase, buffer, ends_from, ends_to):
        copies = []
        for n, step in enumerate(PEERS):
            layer, gx, gy = step
            if gy:
                source = ends_from.at[0 if gy > 0 else 1]
                target = ends_to.at[layer, 0 if gy > 0 else 1, 1 - gx]
            elif gx > 0:
                source, target = buffer.at[0, pl.ds(COLS, RIM)], buffer.at[layer, pl.ds(0, RIM)]
            elif gx < 0:
                source = buffer.at[0, pl.ds(RIM, RIM)]
                target = buffer.at[layer, pl.ds(RIM + COLS, RIM)]
            else:
                source, target = buffer.at[0, pl.ds(RIM, COLS)], buffer.at[1, pl.ds(RIM, COLS)]
            copy = pltpu.make_async_remote_copy(
                src_ref=source,
                dst_ref=target,
                send_sem=send_sem.at[phase, n],
                recv_sem=recv_sem.at[phase, n],
                device_id=peer(step),
                device_id_type=MESH,
            )
            copy.start()
            copies.append(copy)
        return copies

    pl.semaphore_wait(barrier, len(PEERS))
    copies = exchange(0, wide, end_out, end_in)
    loads[3].wait()
    to_columns(prev_in, prev_t, ROWS, 0)
    for copy in copies:
        copy.wait()

    def rim_of(col):
        side = jnp.where(col < RIM, 0, jnp.where(col < RIM + COLS, 1, 2))
        return side, lax.rem(col + COLS - RIM, COLS)

    def end_levels(low, high, k):
        picked = jnp.where(((lane + (124 - 4 * k)) & 127) < 64, high, low)
        return pltpu.roll(picked, 124 - 4 * k, 1)

    def shifted(value, rim, step):
        if step > 0:
            value = jnp.where(lane[: value.shape[0]] < step, rim, value)
        if step < 0:
            value = jnp.where(lane[: value.shape[0]] >= 128 + step, rim, value)
        return pltpu.roll(value, (-step) % 128, 1) if step else value

    def spot_step(t, carry):
        layer, col = t // WIDE, lax.rem(t, WIDE)
        side, own = rim_of(col)
        rim = end_levels(end_in[layer, 0, side, 8:16, :], end_in[layer, 1, side, 8:16, :], own)
        here = wide[layer, col, ROWS:FULL, :]
        for axis in range(2):
            spot[layer, axis, pl.ds(col, 1), :] = here[axis : axis + 1]
            spot_rim[layer, axis, pl.ds(col, 1), :] = rim[axis : axis + 1]
        return carry

    for layer in range(2):
        for axis in range(2):
            spot[layer, axis, 8:16, :] = zero
            spot_rim[layer, axis, 8:16, :] = zero
    lax.fori_loop(0, 2 * WIDE, spot_step, 0)

    layer_id = lax.axis_index("layer")
    cos_t, sin_t = math.cos(twist_angle), math.sin(twist_angle)
    upper = layer_id == 1
    cos_own = jnp.where(upper, jnp.float32(cos_t), jnp.float32(1.0))
    sin_own = jnp.where(upper, jnp.float32(sin_t), jnp.float32(0.0))

    row16 = lax.broadcasted_iota(jnp.int32, (16, 128), 0)
    lane16 = lax.broadcasted_iota(jnp.int32, (16, 128), 1)
    atom = lane16 & 3
    block = (lax.axis_index("gx") * 2 + (row16 + RIM) // 4 - 1 + 2 * lax.axis_size("gx")) % (
        2 * lax.axis_size("gx")
    )
    at_x = (
        ((row16 + RIM) & 3).astype(jnp.float32) * root_three
        + pick(atom, atom_x)
        - cell_w / 2.0
        + cell_w * ((block % PATCH_X).astype(jnp.float32) - (PATCH_X - 1) / 2.0)
    )
    at_y = (
        ((lane16 // 4) & 7).astype(jnp.float32) * 3.0
        + pick(atom, atom_y)
        - cell_h / 2.0
        + cell_h * ((lane16 // 32).astype(jnp.float32) - (PATCH_Y - 1) / 2.0)
    )
    turn_x = (cos_t - 1.0) * at_x - sin_t * at_y
    turn_y = sin_t * at_x + (cos_t - 1.0) * at_y
    own_on = jnp.where(upper, jnp.float32(1.0), jnp.float32(0.0))
    other_on = 1.0 - own_on

    def unturned(ref):
        return (
            cos_own * ref[0, 0] + sin_own * ref[0, 1],
            cos_own * ref[0, 1] - sin_own * ref[0, 0],
        )

    plane_here, plane_rim = unturned(spot), unturned(spot_rim)
    turns = (turn_x, turn_y)
    lane_all = lane16
    for axis in range(2):
        inter_here = spot[1, axis] + other_on * turns[axis]
        inter_rim = spot_rim[1, axis] + other_on * turns[axis]
        for step in range(-STEPS, STEPS + 1):
            for here, rim, target in (
                (plane_here[axis], plane_rim[axis], near_plane),
                (inter_here, inter_rim, near_inter),
            ):
                value = here
                if step > 0:
                    value = jnp.where(lane_all < step, rim, value)
                if step < 0:
                    value = jnp.where(lane_all >= 128 + step, rim, value)
                if step:
                    value = pltpu.roll(value, (-step) % 128, 1)
                target[axis, step + STEPS] = value
        spot[0, axis] = spot[0, axis] + own_on * turns[axis]

    inner = slice(RIM, RIM + COLS)
    own_plane = [near_plane[axis, STEPS, inner, :] for axis in range(2)]
    own_inter = [spot[0, axis, inner, :] for axis in range(2)]

    def atom_heights(index):
        return (index >> 2).astype(jnp.float32) * 3.0 + pick(index & 3, atom_y)

    log2e = 1.0 / math.log(2.0)
    inverse_cut = 1.0 / (cut_radius * cut_radius)
    scale = 2.0 / hop_scale
    sigma_part = v_sigma * math.exp((layer_gap - 1.0) / decay_len)

    def parts(own, near, col, step):
        base_x = pick(lane & 3, atom_x) - pick((lane + step + 8) & 3, atom_x)
        base_y = atom_heights(lane + 8) - atom_heights(lane + (step + 8))
        rows = slice(RIM + col, RIM + col + COLS)
        delta_x = (own[0] - near[0, step + STEPS, rows, :]) + (base_x - col * root_three)
        delta_y = (own[1] - near[1, step + STEPS, rows, :]) + base_y
        return delta_x * delta_x + delta_y * delta_y

    def envelope(dist_sq, inverse):
        spread = dist_sq * inverse
        fall = jnp.exp2(spread * (-log2e / decay_len) + log2e / decay_len)
        scaled = dist_sq * inverse_cut
        return fall * jnp.maximum(1.0 - scaled * scaled, 0.0)

    for n, (col, step) in enumerate(PLANE):
        dist_sq = parts(own_plane, near_plane, col, step)
        hop_plane[n] = envelope(dist_sq, lax.rsqrt(dist_sq)) * (v_pi * scale)
    for n, (col, step) in enumerate(INTER):
        dist_sq = parts(own_inter, near_inter, col, step) + layer_gap * layer_gap
        inverse = lax.rsqrt(dist_sq)
        cosine_sq = (inverse * inverse) * (layer_gap * layer_gap)
        mix = cosine_sq * ((sigma_part - v_pi) * scale) + v_pi * scale
        hop_inter[n] = envelope(dist_sq, inverse) * mix

    def shift_columns(buffer, ends):
        def step_of(t, carry):
            layer, col = t // WIDE, lax.rem(t, WIDE)
            side, own = rim_of(col)
            low, high = ends[layer, 0, side, 0:8, :], ends[layer, 1, side, 0:8, :]
            for g in range(4):
                rim = end_levels(low, high, own * 4 + g)
                here = buffer[layer, col, 8 * g : 8 * g + 8, :]
                for step in range(-STEPS, STEPS + 1):
                    rolled[layer, step + STEPS, col, 8 * g : 8 * g + 8, :] = shifted(here, rim, step)
            return carry

        lax.fori_loop(0, 2 * WIDE, step_of, 0)

    def apply(buffer, minus, minus_first, target, target_first):
        def column(col, carry):
            onsite = wide[0, col + RIM, ROWS + 2 : ROWS + 3, :] * scale
            total = [
                onsite * buffer[0, col + RIM, 8 * g : 8 * g + 8, :]
                - minus[col + minus_first, 8 * g : 8 * g + 8, :]
                for g in range(4)
            ]
            for layer, (offsets, hops) in enumerate(((PLANE, hop_plane), (INTER, hop_inter))):
                for n, (dcol, step) in enumerate(offsets):
                    weight = jnp.broadcast_to(hops[n, pl.ds(col, 1), :], (8, 128))
                    for g in range(4):
                        near = rolled[layer, step + STEPS, col + RIM + dcol, 8 * g : 8 * g + 8, :]
                        total[g] = total[g] + weight * near
            for g in range(4):
                target[col + target_first, 8 * g : 8 * g + 8, :] = total[g]
            return carry

        lax.fori_loop(0, COLS, column, 0)

    def to_blocks(source, first, target):
        for x in range(2):
            for g in range(ROWS // 8):
                columns = [source[first + 4 * x + i, 8 * g : 8 * g + 8, :] for i in range(4)]
                for y, value in enumerate(regroup(columns, lane)):
                    target[0, x, y, 8 * g : 8 * g + 8, :] = value

    shift_columns(wide, end_in)
    apply(wide, prev_t, 0, wide2.at[0], RIM)
    pack_ends(wide2, end_out2, False)
    copies = exchange(1, wide2, end_out2, end_in2)
    to_blocks(wide2.at[0], RIM, first_ref)
    for copy in copies:
        copy.wait()
    shift_columns(wide2, end_in2)
    apply(wide2, wide.at[0], RIM, prev_t, 0)
    to_blocks(prev_t, 0, second_ref)


def body(prev_vec, cur_vec, displace, potential):
    f32 = jnp.float32
    vmem = pl.BlockSpec(memory_space=pltpu.VMEM)
    return pl.pallas_call(
        kernel,
        out_shape=(jax.ShapeDtypeStruct(cur_vec.shape, f32),) * 2,
        in_specs=[pl.BlockSpec(memory_space=pl.ANY)] * 4,
        out_specs=(vmem, vmem),
        scratch_shapes=[
            pltpu.VMEM(prev_vec.shape, f32),
            pltpu.VMEM(cur_vec.shape, f32),
            pltpu.VMEM(displace.shape, f32),
            pltpu.VMEM(potential.shape, f32),
            pltpu.VMEM((2, 4, 8, 128), f32),
            pltpu.VMEM((COLS, ROWS, 128), f32),
            pltpu.VMEM((2, WIDE, FULL, 128), f32),
            pltpu.VMEM((2, WIDE, ROWS, 128), f32),
            pltpu.VMEM((2, 16, 128), f32),
            pltpu.VMEM((2, 2, 3, 16, 128), f32),
            pltpu.VMEM((2, 8, 128), f32),
            pltpu.VMEM((2, 2, 3, 8, 128), f32),
            pltpu.VMEM((2, 2 * STEPS + 1, WIDE, ROWS, 128), f32),
            pltpu.VMEM((2, 2, 16, 128), f32),
            pltpu.VMEM((2, 2, 16, 128), f32),
            pltpu.VMEM((2, 2 * STEPS + 1, 16, 128), f32),
            pltpu.VMEM((2, 2 * STEPS + 1, 16, 128), f32),
            pltpu.VMEM((len(PLANE), COLS, 128), f32),
            pltpu.VMEM((len(INTER), COLS, 128), f32),
            pltpu.SemaphoreType.DMA((4,)),
            pltpu.SemaphoreType.DMA((2, len(PEERS))),
            pltpu.SemaphoreType.DMA((2, len(PEERS))),
        ],
        compiler_params=pltpu.CompilerParams(
            collective_id=0, has_side_effects=True, vmem_limit_bytes=24 * 1024 * 1024
        ),
        name="two_terms",
    )(prev_vec, cur_vec, displace, potential)


def solution(mesh):
    in_specs = (
        P("layer", "gx", "gy", None, None),
        P("layer", "gx", "gy", None, None),
        P("layer", "gx", "gy", None, None),
        P("layer", "gx", "gy", None),
    )
    out_specs = (P("layer", "gx", "gy", None, None), P("layer", "gx", "gy", None, None))
    return jax.shard_map(body, mesh=mesh, in_specs=in_specs, out_specs=out_specs, check_vma=False)
```

```python
import math

import jax
import jax.numpy as jnp
import numpy as np
from jax import lax
from jax.experimental import pallas as pl
from jax.experimental.pallas import tpu as pltpu
from jax.sharding import PartitionSpec as P

MESH = pl.DeviceIdType.MESH
PATCH_X = 14
PATCH_Y = 4

v_pi = -2.7
v_sigma = 0.48
decay_len = 0.319
layer_gap = 3.35 / 1.42
cut_radius = 3.5
hop_scale = 12.0
twist_angle = 1.05 * math.pi / 180.0
root_three = math.sqrt(3.0)
cell_w = 4.0 * root_three
cell_h = 24.0
reach = 0.15

COLS = 8
RIM = 2
WIDE = COLS + 2 * RIM
STEPS = 5
ROWS = 32
GROUP = 4
atom_x = (0.0, root_three / 2.0, root_three / 2.0, 0.0)
atom_y = (0.0, 0.5, 1.5, 2.0)


def near_offsets():
    cos_t, sin_t = math.cos(twist_angle), math.sin(twist_angle)
    cells = []
    for s in range(4):
        col, row = np.meshgrid(np.arange(4 * PATCH_X), np.arange(8 * PATCH_Y), indexing="ij")
        x = (col - 2 * PATCH_X) * root_three + atom_x[s]
        y = (row - 4 * PATCH_Y) * 3.0 + atom_y[s]
        cells.append(np.stack([x.ravel(), y.ravel()], -1))
    places = np.concatenate(cells)
    turn = np.array([[cos_t - 1.0, -sin_t], [sin_t, cos_t - 1.0]])
    drift = places @ turn.T
    drift = np.concatenate([drift, -drift])
    slack = 2.0 * reach + 1e-3
    flat = math.sqrt(cut_radius**2 - layer_gap**2)
    plane, inter = [], []
    for step in range(-STEPS - 2, STEPS + 3):
        for col in range(-RIM - 2, RIM + 3):
            hit_plane = hit_inter = False
            for s in range(4):
                t = (s + step) % 4
                x = atom_x[s] - atom_x[t] - col * root_three
                y = atom_y[s] - atom_y[t] - 3.0 * ((s + step) // 4)
                hit_plane |= math.hypot(x, y) - slack * math.sqrt(2.0) < cut_radius
                gap = np.maximum(np.abs(np.array([x, y]) + drift) - slack, 0.0)
                hit_inter |= bool((np.hypot(gap[:, 0], gap[:, 1]) < flat).any())
            if hit_plane and (col, step) != (0, 0):
                plane.append((col, step))
            if hit_inter:
                inter.append((col, step))
    assert max(abs(c) for c, _ in plane + inter) <= RIM
    assert max(abs(s) for _, s in plane + inter) <= STEPS
    return plane, inter


PLANE, INTER = near_offsets()
TILE = (1, 0, 0)
SIDES = [(a, b, 0) for a in (0, 1) for b in (-1, 1)]
ENDS = [(a, 0, c) for a in (0, 1) for c in (-1, 1)]
CORNERS = [(a, b, c) for a in (0, 1) for b in (-1, 1) for c in (-1, 1)]
PEERS = SIDES + [TILE] + ENDS
MESSAGES = 40
VMEM_LIMIT = 62 * 1024 * 1024


def peer(step):
    sizes = [lax.axis_size(a) for a in ("layer", "gx", "gy")]
    return tuple(
        lax.rem(lax.axis_index(a) + s + n, n) for a, s, n in zip(("layer", "gx", "gy"), step, sizes)
    )


def pick(index, table):
    value = jnp.full(index.shape, table[3], jnp.float32)
    for s in range(3):
        value = jnp.where(index == s, jnp.float32(table[s]), value)
    return value


def regroup(parts, lane):
    group = lane // 32
    results = []
    for a in range(4):
        value = parts[a]
        for b in range(4):
            if b != a:
                value = jnp.where(group == b, pltpu.roll(parts[b], (32 * (b - a)) % 128, 1), value)
        results.append(value)
    return results


def kernel(
    prev_hbm, cur_hbm, disp_hbm, pot_hbm, result,
    prev_in, cur_in, disp_in, pot_in, pot_t, prev_t, second_t, wide, wide2,
    end_out, end_in, end_out2, end_in2, spot_in,
    rims, spot, spot_rim, near_plane, near_inter, own_spot, hop_plane, hop_inter,
    load_sem, send_sem, recv_sem,
):
    barrier = pltpu.get_barrier_semaphore()
    for step in PEERS:
        pl.semaphore_signal(barrier, inc=1, device_id=peer(step), device_id_type=MESH)
    loads = [
        pltpu.make_async_copy(src, dst, load_sem.at[i])
        for i, (src, dst) in enumerate(
            ((disp_hbm, disp_in), (cur_hbm, cur_in), (prev_hbm, prev_in), (pot_hbm, pot_in))
        )
    ]
    for load in loads:
        load.start()
    lane = lax.broadcasted_iota(jnp.int32, (8, 128), 1)
    zero = jnp.zeros((8, 128), jnp.float32)
    sent = []

    def send(source, target, step):
        n = len(sent)
        copy = pltpu.make_async_remote_copy(
            src_ref=source,
            dst_ref=target,
            send_sem=send_sem.at[n],
            recv_sem=recv_sem.at[n],
            device_id=peer(step),
            device_id_type=MESH,
        )
        copy.start()
        sent.append(copy)
        return copy

    def send_side(buffer, layer, gx):
        source, target = (COLS, 0) if gx > 0 else (RIM, RIM + COLS)
        return send(
            buffer.at[0, pl.ds(source, RIM)], buffer.at[layer, pl.ds(target, RIM)], (layer, gx, 0)
        )

    def send_tile(buffer, first, count):
        where = pl.ds(RIM + first, count)
        return send(buffer.at[0, where], buffer.at[1, where], TILE)

    def send_end(source, target, step):
        layer, gx, gy = step
        end = 0 if gy > 0 else 1
        return send(source.at[end], target.at[1 - gx, layer, end], step)

    def to_columns(source, target, first):
        for x in range(2):
            for g in range(ROWS // 8):
                parts = [source[0, x, y, 8 * g : 8 * g + 8, :] for y in range(4)]
                for i, value in enumerate(regroup(parts, lane)):
                    target[first + 4 * x + i, 8 * g : 8 * g + 8, :] = value

    def pack_ends(source, target):
        low, high = zero, zero
        for k in range(32):
            value = source[0, RIM + k // 4, 8 * (k % 4) : 8 * (k % 4) + 8, :]
            value = pltpu.roll(value, (4 * k + 4) % 128, 1)
            low = jnp.where(lane // 4 == k, value, low)
            high = jnp.where(lane // 4 == (k + 1) % 32, value, high)
        target[0, 0:8, :] = low
        target[1, 0:8, :] = high

    loads[0].wait()
    for x in range(2):
        for i, value in enumerate(regroup([disp_in[0, x, y] for y in range(4)], lane[:2])):
            for axis in range(2):
                spot_in[1, 0, axis, 4 * x + i : 4 * x + i + 1, :] = value[axis : axis + 1]
    for end in range(2):
        end_out[end, 8:16, :] = spot_in[1, 0, 0]
        end_out[end, 16:24, :] = spot_in[1, 0, 1]
    loads[1].wait()
    to_columns(cur_in, wide.at[0], RIM)
    pack_ends(wide, end_out)

    pl.semaphore_wait(barrier, len(PEERS))
    ends = [send_end(end_out, end_in, step) for step in ENDS]
    spots = [send(spot_in.at[1, 0], spot_in.at[1 - gx, layer], (layer, gx, gy)) for layer, gx, gy in SIDES + [TILE]]
    right_rim = [send_side(wide, layer, -1) for layer in (1, 0)]
    right_tile = send_tile(wide, 2, COLS - 2)
    left_rim = [send_side(wide, layer, 1) for layer in (1, 0)]
    left_tile = send_tile(wide, 0, 2)

    loads[2].wait()
    to_columns(prev_in, prev_t, 0)
    loads[3].wait()
    for x in range(2):
        for i, value in enumerate(regroup([pot_in[0, x, y : y + 1] for y in range(4)], lane[:1])):
            pot_t[4 * x + i : 4 * x + i + 1, :] = value

    for copy in ends:
        copy.wait_recv()
    corners = [send(end_in.at[1], end_in.at[1 - gx], (0, gx, 0)) for gx in (-1, 1)]
    for copy in spots + corners:
        copy.wait_recv()

    def rim_of(col):
        side = 0 if col < RIM else (1 if col < RIM + COLS else 2)
        return side, (col + COLS - RIM) % COLS

    def end_levels(low, high, k):
        picked = jnp.where(((lane + (124 - 4 * k)) & 127) < 64, high, low)
        return pltpu.roll(picked, 124 - 4 * k, 1)

    def with_rim(sides):
        return jnp.concatenate([sides[0][COLS - RIM :], sides[1], sides[2][:RIM], zero[:4]], axis=0)

    for layer in range(2):
        for axis in range(2):
            spot[layer, axis] = with_rim([spot_in[side, layer, axis] for side in range(3)])
            rows = slice(8 + 8 * axis, 16 + 8 * axis)
            spot_rim[layer, axis] = with_rim([
                jnp.where(lane < 64, end_in[side, layer, 1, rows, :], end_in[side, layer, 0, rows, :])
                for side in range(3)
            ])

    layer_id = lax.axis_index("layer")
    cos_t, sin_t = math.cos(twist_angle), math.sin(twist_angle)
    upper = layer_id == 1
    cos_own = jnp.where(upper, jnp.float32(cos_t), jnp.float32(1.0))
    sin_own = jnp.where(upper, jnp.float32(sin_t), jnp.float32(0.0))

    row16 = lax.broadcasted_iota(jnp.int32, (16, 128), 0)
    lane16 = lax.broadcasted_iota(jnp.int32, (16, 128), 1)
    atom = lane16 & 3
    block = (lax.axis_index("gx") * 2 + (row16 + RIM) // 4 - 1 + 2 * lax.axis_size("gx")) % (
        2 * lax.axis_size("gx")
    )
    at_x = (
        ((row16 + RIM) & 3).astype(jnp.float32) * root_three
        + pick(atom, atom_x)
        - cell_w / 2.0
        + cell_w * ((block % PATCH_X).astype(jnp.float32) - (PATCH_X - 1) / 2.0)
    )
    at_y = (
        ((lane16 // 4) & 7).astype(jnp.float32) * 3.0
        + pick(atom, atom_y)
        - cell_h / 2.0
        + cell_h * ((lane16 // 32).astype(jnp.float32) - (PATCH_Y - 1) / 2.0)
    )
    turn_x = (cos_t - 1.0) * at_x - sin_t * at_y
    turn_y = sin_t * at_x + (cos_t - 1.0) * at_y
    own_on = jnp.where(upper, jnp.float32(1.0), jnp.float32(0.0))
    other_on = 1.0 - own_on

    def unturned(ref):
        return (
            cos_own * ref[0, 0] + sin_own * ref[0, 1],
            cos_own * ref[0, 1] - sin_own * ref[0, 0],
        )

    plane_here, plane_rim = unturned(spot), unturned(spot_rim)
    turns = (turn_x, turn_y)

    def joined(here, rim, step, lanes):
        if step > 0:
            return jnp.where(lanes < step, rim, here)
        if step < 0:
            return jnp.where(lanes >= 128 + step, rim, here)
        return here

    def rolled_by(value, step):
        return pltpu.roll(value, step % 128, 1) if step else value

    inner = slice(RIM, RIM + COLS)
    for axis in range(2):
        near_plane[axis, 0] = plane_here[axis]
        near_plane[axis, 1] = plane_rim[axis]
        near_inter[axis, 0] = spot[1, axis] + other_on * turns[axis]
        near_inter[axis, 1] = spot_rim[1, axis] + other_on * turns[axis]
        own_spot[axis] = near_plane[axis, 0, inner, :]
        own_spot[2 + axis] = spot[0, axis, inner, :] + own_on * turns[axis][inner]

    def atom_heights(index):
        return (index >> 2).astype(jnp.float32) * 3.0 + pick(index & 3, atom_y)

    log2e = 1.0 / math.log(2.0)
    inverse_cut = 1.0 / (cut_radius * cut_radius)
    scale = 2.0 / hop_scale
    sigma_part = v_sigma * math.exp((layer_gap - 1.0) / decay_len)

    def parts(first, near, col, step):
        base_x = pick((lane - step + 8) & 3, atom_x) - pick(lane & 3, atom_x)
        base_y = atom_heights(lane - step + 8) - atom_heights(lane + 8)
        rows = slice(RIM + col, RIM + col + COLS)
        own = [rolled_by(own_spot[first + axis], step) for axis in range(2)]
        other = [joined(near[axis, 0, rows, :], near[axis, 1, rows, :], step, lane) for axis in range(2)]
        delta_x = (own[0] - other[0]) + (base_x - col * root_three)
        delta_y = (own[1] - other[1]) + base_y
        return delta_x * delta_x + delta_y * delta_y

    def envelope(dist_sq, inverse):
        spread = dist_sq * inverse
        fall = jnp.exp2(spread * (-log2e / decay_len) + log2e / decay_len)
        scaled = dist_sq * inverse_cut
        return fall * jnp.maximum(1.0 - scaled * scaled, 0.0)

    for n, (col, step) in enumerate(PLANE):
        dist_sq = parts(0, near_plane, col, step)
        hop_plane[n] = envelope(dist_sq, lax.rsqrt(dist_sq)) * (v_pi * scale)
    for n, (col, step) in enumerate(INTER):
        dist_sq = parts(2, near_inter, col, step) + layer_gap * layer_gap
        inverse = lax.rsqrt(dist_sq)
        cosine_sq = (inverse * inverse) * (layer_gap * layer_gap)
        mix = cosine_sq * ((sigma_part - v_pi) * scale) + v_pi * scale
        hop_inter[n] = envelope(dist_sq, inverse) * mix

    def unpack_ends(ends):
        for layer in range(2):
            for col in range(WIDE):
                side, own = rim_of(col)
                for g in range(4):
                    low, high = ends[side, layer, 0, 0:8, :], ends[side, layer, 1, 0:8, :]
                    rims[layer, col, 8 * g : 8 * g + 8, :] = end_levels(low, high, own * 4 + g)

    def apply(buffer, minus, minus_first, target, target_first, first, count):
        def columns(group, carry):
            base = group * GROUP
            total = {}
            for d in range(GROUP):
                onsite = jnp.broadcast_to(pot_t[pl.ds(base + d, 1), :] * scale, (8, 128))
                for g in range(4):
                    rows = slice(8 * g, 8 * g + 8)
                    total[d, g] = (
                        onsite * buffer[0, base + d + RIM, rows, :] - minus[base + d + minus_first, rows, :]
                    )
            for step in range(-STEPS, STEPS + 1):
                part = {}
                for layer, (offsets, hops) in enumerate(((PLANE, hop_plane), (INTER, hop_inter))):
                    here = [(n, dcol) for n, (dcol, s) in enumerate(offsets) if s == step]
                    weight = {
                        (n, d): jnp.broadcast_to(hops[n, pl.ds(base + d, 1), :], (8, 128))
                        for n, _ in here
                        for d in range(GROUP)
                    }
                    for c in range(GROUP + 2 * RIM):
                        users = [(n, c - RIM - dcol) for n, dcol in here if 0 <= c - RIM - dcol < GROUP]
                        for g in range(4):
                            rows = slice(8 * g, 8 * g + 8)
                            near = buffer[layer, base + c, rows, :]
                            if step:
                                near = joined(near, rims[layer, base + c, rows, :], step, lane)
                            for n, d in users:
                                term = weight[n, d] * near
                                part[d, g] = part[d, g] + term if (d, g) in part else term
                for key, value in part.items():
                    total[key] = total[key] + rolled_by(value, -step)
            for (d, g), value in total.items():
                target[base + d + target_first, 8 * g : 8 * g + 8, :] = value
            return carry

        lax.fori_loop(first // GROUP, (first + count) // GROUP, columns, 0)

    def to_blocks(source, first, n):
        for x in range(2):
            for g in range(ROWS // 8):
                columns = [source[first + 4 * x + i, 8 * g : 8 * g + 8, :] for i in range(4)]
                for y, value in enumerate(regroup(columns, lane)):
                    result[n, 0, x, y, 8 * g : 8 * g + 8, :] = value

    half = COLS // 2
    unpack_ends(end_in)
    for copy in right_rim + [right_tile]:
        copy.wait_recv()
    apply(wide, prev_t, 0, wide2.at[0], RIM, half, half)
    last = [send_side(wide2, layer, 1) for layer in (1, 0)]
    last.append(send_tile(wide2, half, half))
    for copy in left_rim + [left_tile]:
        copy.wait_recv()
    apply(wide, prev_t, 0, wide2.at[0], RIM, 0, half)
    pack_ends(wide2, end_out2)
    last += [send_end(end_out2, end_in2, step) for step in ENDS + CORNERS]
    last += [send_side(wide2, layer, -1) for layer in (1, 0)]
    last.append(send_tile(wide2, 0, half))
    to_blocks(wide2.at[0], RIM, 0)
    for copy in last:
        copy.wait_recv()
    unpack_ends(end_in2)
    apply(wide2, wide.at[0], RIM, second_t, 0, 0, COLS)
    to_blocks(second_t, 0, 1)
    for copy in sent:
        copy.wait_send()


def finish(result, first_ref, second_ref):
    first_ref[...] = result[0]
    second_ref[...] = result[1]


def body(prev_vec, cur_vec, displace, potential):
    f32 = jnp.float32
    near = pltpu.VMEM((2, 2, 16, 128), f32)
    hbm, vmem = pl.BlockSpec(memory_space=pltpu.HBM), pl.BlockSpec(memory_space=pltpu.VMEM)
    result = pl.pallas_call(
        kernel,
        out_shape=jax.ShapeDtypeStruct((2,) + cur_vec.shape, f32),
        in_specs=[hbm] * 4,
        out_specs=pl.BlockSpec(memory_space=pltpu.VMEM),
        scratch_shapes=[
            pltpu.VMEM(prev_vec.shape, f32),
            pltpu.VMEM(cur_vec.shape, f32),
            pltpu.VMEM(displace.shape, f32),
            pltpu.VMEM(potential.shape, f32),
            pltpu.VMEM((COLS, 128), f32),
            pltpu.VMEM((COLS, ROWS, 128), f32),
            pltpu.VMEM((COLS, ROWS, 128), f32),
            pltpu.VMEM((2, WIDE, ROWS, 128), f32),
            pltpu.VMEM((2, WIDE, ROWS, 128), f32),
            pltpu.VMEM((2, 24, 128), f32),
            pltpu.VMEM((3, 2, 2, 24, 128), f32),
            pltpu.VMEM((2, 8, 128), f32),
            pltpu.VMEM((3, 2, 2, 8, 128), f32),
            pltpu.VMEM((3, 2, 2, COLS, 128), f32),
            pltpu.VMEM((2, WIDE, ROWS, 128), f32),
            near,
            near,
            near,
            near,
            pltpu.VMEM((4, COLS, 128), f32),
            pltpu.VMEM((len(PLANE), COLS, 128), f32),
            pltpu.VMEM((len(INTER), COLS, 128), f32),
            pltpu.SemaphoreType.DMA((4,)),
            pltpu.SemaphoreType.DMA((MESSAGES,)),
            pltpu.SemaphoreType.DMA((MESSAGES,)),
        ],
        compiler_params=pltpu.CompilerParams(
            collective_id=0, has_side_effects=True, vmem_limit_bytes=VMEM_LIMIT
        ),
        name="two_terms",
    )(prev_vec, cur_vec, displace, potential)
    return pl.pallas_call(
        finish,
        out_shape=(jax.ShapeDtypeStruct(cur_vec.shape, f32),) * 2,
        in_specs=[vmem],
        out_specs=(vmem, vmem),
        name="finish",
    )(result)


def solution(mesh):
    in_specs = (
        P("layer", "gx", "gy", None, None),
        P("layer", "gx", "gy", None, None),
        P("layer", "gx", "gy", None, None),
        P("layer", "gx", "gy", None),
    )
    out_specs = (P("layer", "gx", "gy", None, None), P("layer", "gx", "gy", None, None))
    return jax.shard_map(body, mesh=mesh, in_specs=in_specs, out_specs=out_specs, check_vma=False)
```

```python
import math

import jax
import jax.numpy as jnp
import numpy as np
from jax import lax
from jax.experimental import pallas as pl
from jax.experimental.pallas import tpu as pltpu
from jax.sharding import PartitionSpec as P

MESH = pl.DeviceIdType.MESH
PATCH_X = 14
PATCH_Y = 4

v_pi = -2.7
v_sigma = 0.48
decay_len = 0.319
layer_gap = 3.35 / 1.42
cut_radius = 3.5
hop_scale = 12.0
twist_angle = 1.05 * math.pi / 180.0
root_three = math.sqrt(3.0)
cell_w = 4.0 * root_three
cell_h = 24.0
reach = 0.15

COLS = 8
RIM = 2
WIDE = COLS + 2 * RIM
STEPS = 5
ROWS = 32
GROUP = 4
atom_x = (0.0, root_three / 2.0, root_three / 2.0, 0.0)
atom_y = (0.0, 0.5, 1.5, 2.0)


def near_offsets():
    cos_t, sin_t = math.cos(twist_angle), math.sin(twist_angle)
    cells = []
    for s in range(4):
        col, row = np.meshgrid(np.arange(4 * PATCH_X), np.arange(8 * PATCH_Y), indexing="ij")
        x = (col - 2 * PATCH_X) * root_three + atom_x[s]
        y = (row - 4 * PATCH_Y) * 3.0 + atom_y[s]
        cells.append(np.stack([x.ravel(), y.ravel()], -1))
    places = np.concatenate(cells)
    turn = np.array([[cos_t - 1.0, -sin_t], [sin_t, cos_t - 1.0]])
    drift = places @ turn.T
    drift = np.concatenate([drift, -drift])
    slack = 2.0 * reach + 1e-3
    flat = math.sqrt(cut_radius**2 - layer_gap**2)
    plane, inter = [], []
    for step in range(-STEPS - 2, STEPS + 3):
        for col in range(-RIM - 2, RIM + 3):
            hit_plane = hit_inter = False
            for s in range(4):
                t = (s + step) % 4
                x = atom_x[s] - atom_x[t] - col * root_three
                y = atom_y[s] - atom_y[t] - 3.0 * ((s + step) // 4)
                hit_plane |= math.hypot(x, y) - slack * math.sqrt(2.0) < cut_radius
                gap = np.maximum(np.abs(np.array([x, y]) + drift) - slack, 0.0)
                hit_inter |= bool((np.hypot(gap[:, 0], gap[:, 1]) < flat).any())
            if hit_plane and (col, step) != (0, 0):
                plane.append((col, step))
            if hit_inter:
                inter.append((col, step))
    assert max(abs(c) for c, _ in plane + inter) <= RIM
    assert max(abs(s) for _, s in plane + inter) <= STEPS
    return plane, inter


PLANE, INTER = near_offsets()
TILE = (1, 0, 0)
SIDES = [(a, b, 0) for a in (0, 1) for b in (-1, 1)]
ENDS = [(a, 0, c) for a in (0, 1) for c in (-1, 1)]
CORNERS = [(a, b, c) for a in (0, 1) for b in (-1, 1) for c in (-1, 1)]
LEFT = [(a, -1, 0) for a in (0, 1)]
RIGHT = [(a, 1, 0) for a in (0, 1)]
PEERS = [TILE] + ENDS
MESSAGES = 41
VMEM_LIMIT = 40 * 1024 * 1024


def peer(step):
    sizes = [lax.axis_size(a) for a in ("layer", "gx", "gy")]
    return tuple(
        lax.rem(lax.axis_index(a) + s + n, n) for a, s, n in zip(("layer", "gx", "gy"), step, sizes)
    )


def pick(index, table):
    value = jnp.full(index.shape, table[3], jnp.float32)
    for s in range(3):
        value = jnp.where(index == s, jnp.float32(table[s]), value)
    return value


def regroup(parts, lane):
    group = lane // 32
    results = []
    for a in range(4):
        value = parts[a]
        for b in range(4):
            if b != a:
                value = jnp.where(group == b, pltpu.roll(parts[b], (32 * (b - a)) % 128, 1), value)
        results.append(value)
    return results


def kernel(
    prev_hbm, cur_hbm, disp_hbm, pot_hbm, result,
    prev_in, cur_in, disp_in, pot_in, pot_t, prev_t, second_t, wide, wide2,
    end_out, end_in, end_out2, end_in2, spot_in,
    rims, spot, spot_rim, near_plane, near_inter, own_spot, hop_plane, hop_inter,
    load_sem, send_sem, recv_sem, corner_sem, left_sem,
):
    barrier = pltpu.get_barrier_semaphore()
    for step in PEERS + LEFT:
        pl.semaphore_signal(barrier, inc=1, device_id=peer(step), device_id_type=MESH)
    loads = [
        pltpu.make_async_copy(src, dst, load_sem.at[i])
        for i, (src, dst) in enumerate(
            ((disp_hbm, disp_in), (cur_hbm, cur_in), (prev_hbm, prev_in), (pot_hbm, pot_in))
        )
    ]
    for load in loads:
        load.start()
    lane = lax.broadcasted_iota(jnp.int32, (8, 128), 1)
    zero = jnp.zeros((8, 128), jnp.float32)
    sent = []

    def send(source, target, step):
        n = len(sent)
        assert n < MESSAGES
        copy = pltpu.make_async_remote_copy(
            src_ref=source,
            dst_ref=target,
            send_sem=send_sem.at[n],
            recv_sem=recv_sem.at[n],
            device_id=peer(step),
            device_id_type=MESH,
        )
        copy.start()
        sent.append(copy)
        return copy

    def send_side(buffer, layer, gx):
        source, target = (COLS, 0) if gx > 0 else (RIM, RIM + COLS)
        return send(
            buffer.at[0, pl.ds(source, RIM)], buffer.at[layer, pl.ds(target, RIM)], (layer, gx, 0)
        )

    def send_tile(buffer, first, count):
        where = pl.ds(RIM + first, count)
        return send(buffer.at[0, where], buffer.at[1, where], TILE)

    def send_end(source, target, step):
        layer, gx, gy = step
        end = 0 if gy > 0 else 1
        return send(source.at[end], target.at[1 - gx, layer, end], step)

    def to_columns(source, target, first):
        for x in range(2):
            for g in range(ROWS // 8):
                parts = [source[0, x, y, 8 * g : 8 * g + 8, :] for y in range(4)]
                for i, value in enumerate(regroup(parts, lane)):
                    target[first + 4 * x + i, 8 * g : 8 * g + 8, :] = value

    def pack_ends(source, targets, columns, ends=None):
        low, high = ends or (zero, zero)
        for k in range(4 * columns.start, 4 * columns.stop):
            value = source[0, RIM + k // 4, 8 * (k % 4) : 8 * (k % 4) + 8, :]
            value = pltpu.roll(value, (4 * k + 4) % 128, 1)
            low = jnp.where(lane // 4 == k, value, low)
            high = jnp.where(lane // 4 == (k + 1) % 32, value, high)
        targets[0, 0:8, :] = low
        targets[1, 0:8, :] = high
        return low, high

    loads[0].wait()
    for x in range(2):
        for i, value in enumerate(regroup([disp_in[0, x, y] for y in range(4)], lane[:2])):
            for axis in range(2):
                spot_in[1, 0, axis, 4 * x + i : 4 * x + i + 1, :] = value[axis : axis + 1]
    for end in range(2):
        moved = pltpu.roll(spot_in[1, 0, 1], 4 if end else 124, 1)
        keep = lane < 4 if end else lane >= 124
        end_out[end, 8:16, :] = jnp.where(keep, spot_in[1, 0, 0], moved)
    loads[1].wait()
    to_columns(cur_in, wide.at[0], RIM)
    pack_ends(wide, end_out, range(COLS))

    def tell(sem, steps):
        for step in steps:
            pl.semaphore_signal(sem, inc=1, device_id=peer(step), device_id_type=MESH)

    def send_spots(steps):
        return [send(spot_in.at[1, 0], spot_in.at[1 - gx, layer], (layer, gx, gy)) for layer, gx, gy in steps]

    pl.semaphore_wait(barrier, len(PEERS + RIGHT))
    tell(left_sem, RIGHT)
    tell(corner_sem.at[0], [(0, 0, -1), (0, 0, 1)])
    near_right = [send_end(end_out, end_in, step) for step in ENDS]
    near_right += send_spots([TILE])
    near_left = send_spots(RIGHT)
    right_tile = send_tile(wide, 2, COLS - 2)
    left_rim = [send_side(wide, layer, 1) for layer in (1, 0)]
    left_tile = send_tile(wide, 0, 2)
    pl.semaphore_wait(corner_sem.at[0], 2)
    near_left += [send_end(end_out, end_in, step) for step in CORNERS if step[1] > 0]
    pl.semaphore_wait(left_sem, 2)
    tell(corner_sem.at[1], [(0, 0, -1), (0, 0, 1)])
    near_right += send_spots(LEFT)
    right_rim = [send_side(wide, layer, -1) for layer in (1, 0)]
    pl.semaphore_wait(corner_sem.at[1], 2)
    near_right += [send_end(end_out, end_in, step) for step in CORNERS if step[1] < 0]

    loads[2].wait()
    to_columns(prev_in, prev_t, 0)
    loads[3].wait()
    for x in range(2):
        for i, value in enumerate(regroup([pot_in[0, x, y : y + 1] for y in range(4)], lane[:1])):
            pot_t[4 * x + i : 4 * x + i + 1, :] = value

    def rim_of(col):
        side = 0 if col < RIM else (1 if col < RIM + COLS else 2)
        return side, (col + COLS - RIM) % COLS

    def end_levels(low, high, k):
        picked = jnp.where(((lane + (124 - 4 * k)) & 127) < 64, high, low)
        return pltpu.roll(picked, 124 - 4 * k, 1)

    def with_rim(sides):
        return jnp.concatenate([sides[0][COLS - RIM :], sides[1], sides[2][:RIM], zero[:4]], axis=0)

    def end_spot(side, layer, axis):
        low, high = end_in[side, layer, 0, 8:16, :], end_in[side, layer, 1, 8:16, :]
        if axis:
            low, high = pltpu.roll(low, 4, 1), pltpu.roll(high, 124, 1)
        return jnp.where(lane < 64, high, low)

    layer_id = lax.axis_index("layer")
    cos_t, sin_t = math.cos(twist_angle), math.sin(twist_angle)
    upper = layer_id == 1
    cos_own = jnp.where(upper, jnp.float32(cos_t), jnp.float32(1.0))
    sin_own = jnp.where(upper, jnp.float32(sin_t), jnp.float32(0.0))

    row16 = lax.broadcasted_iota(jnp.int32, (16, 128), 0)
    lane16 = lax.broadcasted_iota(jnp.int32, (16, 128), 1)
    atom = lane16 & 3
    block = (lax.axis_index("gx") * 2 + (row16 + RIM) // 4 - 1 + 2 * lax.axis_size("gx")) % (
        2 * lax.axis_size("gx")
    )
    at_x = (
        ((row16 + RIM) & 3).astype(jnp.float32) * root_three
        + pick(atom, atom_x)
        - cell_w / 2.0
        + cell_w * ((block % PATCH_X).astype(jnp.float32) - (PATCH_X - 1) / 2.0)
    )
    at_y = (
        ((lane16 // 4) & 7).astype(jnp.float32) * 3.0
        + pick(atom, atom_y)
        - cell_h / 2.0
        + cell_h * ((lane16 // 32).astype(jnp.float32) - (PATCH_Y - 1) / 2.0)
    )
    turn_x = (cos_t - 1.0) * at_x - sin_t * at_y
    turn_y = sin_t * at_x + (cos_t - 1.0) * at_y
    own_on = jnp.where(upper, jnp.float32(1.0), jnp.float32(0.0))
    other_on = 1.0 - own_on

    def unturned(ref):
        return (
            cos_own * ref[0, 0] + sin_own * ref[0, 1],
            cos_own * ref[0, 1] - sin_own * ref[0, 0],
        )

    turns = (turn_x, turn_y)

    def joined(here, rim, step, lanes):
        if step > 0:
            return jnp.where(lanes < step, rim, here)
        if step < 0:
            return jnp.where(lanes >= 128 + step, rim, here)
        return here

    def rolled_by(value, step):
        return pltpu.roll(value, step % 128, 1) if step else value

    inner = slice(RIM, RIM + COLS)
    def find_spots(sides):
        blank = [zero] * 3
        for layer in range(2):
            for axis in range(2):
                here, rim = list(blank), list(blank)
                for side in sides:
                    here[side] = spot_in[side, layer, axis]
                    rim[side] = end_spot(side, layer, axis)
                spot[layer, axis] = with_rim(here)
                spot_rim[layer, axis] = with_rim(rim)
        plane_here, plane_rim = unturned(spot), unturned(spot_rim)
        for axis in range(2):
            near_plane[axis, 0] = plane_here[axis]
            near_plane[axis, 1] = plane_rim[axis]
            near_inter[axis, 0] = spot[1, axis] + other_on * turns[axis]
            near_inter[axis, 1] = spot_rim[1, axis] + other_on * turns[axis]
            own_spot[axis] = near_plane[axis, 0, inner, :]
            own_spot[2 + axis] = spot[0, axis, inner, :] + own_on * turns[axis][inner]

    def atom_heights(index):
        return (index >> 2).astype(jnp.float32) * 3.0 + pick(index & 3, atom_y)

    log2e = 1.0 / math.log(2.0)
    inverse_cut = 1.0 / (cut_radius * cut_radius)
    scale = 2.0 / hop_scale
    sigma_part = v_sigma * math.exp((layer_gap - 1.0) / decay_len)

    def parts(first, near, col, step):
        base_x = pick((lane - step + 8) & 3, atom_x) - pick(lane & 3, atom_x)
        base_y = atom_heights(lane - step + 8) - atom_heights(lane + 8)
        rows = slice(RIM + col, RIM + col + COLS)
        own = [rolled_by(own_spot[first + axis], step) for axis in range(2)]
        other = [joined(near[axis, 0, rows, :], near[axis, 1, rows, :], step, lane) for axis in range(2)]
        delta_x = (own[0] - other[0]) + (base_x - col * root_three)
        delta_y = (own[1] - other[1]) + base_y
        return delta_x * delta_x + delta_y * delta_y

    def envelope(dist_sq, inverse):
        spread = dist_sq * inverse
        fall = jnp.exp2(spread * (-log2e / decay_len) + log2e / decay_len)
        scaled = dist_sq * inverse_cut
        return fall * jnp.maximum(1.0 - scaled * scaled, 0.0)

    def find_hops():
        for n, (col, step) in enumerate(PLANE):
            dist_sq = parts(0, near_plane, col, step)
            hop_plane[n] = envelope(dist_sq, lax.rsqrt(dist_sq)) * (v_pi * scale)
        for n, (col, step) in enumerate(INTER):
            dist_sq = parts(2, near_inter, col, step) + layer_gap * layer_gap
            inverse = lax.rsqrt(dist_sq)
            cosine_sq = (inverse * inverse) * (layer_gap * layer_gap)
            mix = cosine_sq * ((sigma_part - v_pi) * scale) + v_pi * scale
            hop_inter[n] = envelope(dist_sq, inverse) * mix

    def unpack_ends(ends, columns):
        for layer in range(2):
            for col in columns:
                side, own = rim_of(col)
                for g in range(4):
                    low, high = ends[side, layer, 0, 0:8, :], ends[side, layer, 1, 0:8, :]
                    rims[layer, col, 8 * g : 8 * g + 8, :] = end_levels(low, high, own * 4 + g)

    def apply(buffer, minus, minus_first, target, target_first, first, count):
        def columns(group, carry):
            base = group * GROUP
            total = {}
            for d in range(GROUP):
                onsite = jnp.broadcast_to(pot_t[pl.ds(base + d, 1), :] * scale, (8, 128))
                for g in range(4):
                    rows = slice(8 * g, 8 * g + 8)
                    total[d, g] = (
                        onsite * buffer[0, base + d + RIM, rows, :] - minus[base + d + minus_first, rows, :]
                    )
            for step in range(-STEPS, STEPS + 1):
                part = {}
                for layer, (offsets, hops) in enumerate(((PLANE, hop_plane), (INTER, hop_inter))):
                    here = [(n, dcol) for n, (dcol, s) in enumerate(offsets) if s == step]
                    weight = {
                        (n, d): jnp.broadcast_to(hops[n, pl.ds(base + d, 1), :], (8, 128))
                        for n, _ in here
                        for d in range(GROUP)
                    }
                    for c in range(GROUP + 2 * RIM):
                        users = [(n, c - RIM - dcol) for n, dcol in here if 0 <= c - RIM - dcol < GROUP]
                        for g in range(4):
                            rows = slice(8 * g, 8 * g + 8)
                            near = buffer[layer, base + c, rows, :]
                            if step:
                                near = joined(near, rims[layer, base + c, rows, :], step, lane)
                            for n, d in users:
                                term = weight[n, d] * near
                                part[d, g] = part[d, g] + term if (d, g) in part else term
                for key, value in part.items():
                    total[key] = total[key] + rolled_by(value, -step)
            for (d, g), value in total.items():
                target[base + d + target_first, 8 * g : 8 * g + 8, :] = value
            return carry

        lax.fori_loop(first // GROUP, (first + count) // GROUP, columns, 0)

    def to_blocks(source, first, n):
        for x in range(2):
            for g in range(ROWS // 8):
                columns = [source[first + 4 * x + i, 8 * g : 8 * g + 8, :] for i in range(4)]
                for y, value in enumerate(regroup(columns, lane)):
                    result[n, 0, x, y, 8 * g : 8 * g + 8, :] = value

    half = COLS // 2
    right_wide, left_wide = range(half, WIDE), range(half)

    def arrive(copies):
        for copy in copies:
            copy.wait_recv()

    arrive(near_right)
    find_spots((1, 2))
    find_hops()
    unpack_ends(end_in, right_wide)
    arrive(right_rim + [right_tile])
    apply(wide, prev_t, 0, wide2.at[0], RIM, half, half)
    tile2 = [send_tile(wide2, half, half)]
    from_left = [send_side(wide2, layer, 1) for layer in (1, 0)]
    packed = pack_ends(wide2, end_out2.at[0], range(half, COLS))
    from_left += [send_end(end_out2.at[0], end_in2, step) for step in CORNERS if step[1] > 0]
    arrive(near_left)
    find_spots((0, 1, 2))
    find_hops()
    unpack_ends(end_in, left_wide)
    arrive(left_rim + [left_tile])
    apply(wide, prev_t, 0, wide2.at[0], RIM, 0, half)
    tile2.append(send_tile(wide2, 0, half))
    from_right = [send_side(wide2, layer, -1) for layer in (1, 0)]
    pack_ends(wide2, end_out2.at[1], range(half), packed)
    from_right += [
        send_end(end_out2.at[1], end_in2, step) for step in ENDS + CORNERS if step[1] <= 0
    ]
    to_blocks(wide2.at[0], RIM, 0)
    for copy in sent:
        copy.wait_send()
    arrive(tile2 + from_right)
    unpack_ends(end_in2, right_wide)
    apply(wide2, wide.at[0], RIM, second_t, 0, half, half)
    arrive(from_left)
    unpack_ends(end_in2, left_wide)
    apply(wide2, wide.at[0], RIM, second_t, 0, 0, half)
    to_blocks(second_t, 0, 1)


def finish(result, first_ref, second_ref, sem):
    copies = [
        pltpu.make_async_copy(result.at[n], target, sem.at[n])
        for n, target in enumerate((first_ref, second_ref))
    ]
    for copy in copies:
        copy.start()
    for copy in copies:
        copy.wait()


def body(prev_vec, cur_vec, displace, potential):
    f32 = jnp.float32
    near = pltpu.VMEM((2, 2, 16, 128), f32)
    hbm, vmem = pl.BlockSpec(memory_space=pltpu.HBM), pl.BlockSpec(memory_space=pltpu.VMEM)
    result = pl.pallas_call(
        kernel,
        out_shape=pltpu.VMEM((2,) + cur_vec.shape, f32),
        in_specs=[hbm] * 4,
        out_specs=pl.BlockSpec(memory_space=pltpu.VMEM),
        scratch_shapes=[
            pltpu.VMEM(prev_vec.shape, f32),
            pltpu.VMEM(cur_vec.shape, f32),
            pltpu.VMEM(displace.shape, f32),
            pltpu.VMEM(potential.shape, f32),
            pltpu.VMEM((COLS, 128), f32),
            pltpu.VMEM((COLS, ROWS, 128), f32),
            pltpu.VMEM((COLS, ROWS, 128), f32),
            pltpu.VMEM((2, WIDE, ROWS, 128), f32),
            pltpu.VMEM((2, WIDE, ROWS, 128), f32),
            pltpu.VMEM((2, 16, 128), f32),
            pltpu.VMEM((3, 2, 2, 16, 128), f32),
            pltpu.VMEM((2, 2, 8, 128), f32),
            pltpu.VMEM((3, 2, 2, 8, 128), f32),
            pltpu.VMEM((3, 2, 2, COLS, 128), f32),
            pltpu.VMEM((2, WIDE, ROWS, 128), f32),
            near,
            near,
            near,
            near,
            pltpu.VMEM((4, COLS, 128), f32),
            pltpu.VMEM((len(PLANE), COLS, 128), f32),
            pltpu.VMEM((len(INTER), COLS, 128), f32),
            pltpu.SemaphoreType.DMA((4,)),
            pltpu.SemaphoreType.DMA((MESSAGES,)),
            pltpu.SemaphoreType.DMA((MESSAGES,)),
            pltpu.SemaphoreType.REGULAR((2,)),
            pltpu.SemaphoreType.REGULAR,
        ],
        compiler_params=pltpu.CompilerParams(
            collective_id=0, has_side_effects=True, vmem_limit_bytes=VMEM_LIMIT
        ),
        name="two_terms",
    )(*[pltpu.with_memory_space_constraint(x, pltpu.HBM) for x in (prev_vec, cur_vec, displace, potential)])
    return pl.pallas_call(
        finish,
        out_shape=(jax.ShapeDtypeStruct(cur_vec.shape, f32),) * 2,
        in_specs=[vmem],
        out_specs=(hbm, hbm),
        scratch_shapes=[
            pltpu.SemaphoreType.DMA((2,)),
        ],
        compiler_params=pltpu.CompilerParams(vmem_limit_bytes=VMEM_LIMIT),
        name="finish",
    )(result)


def solution(mesh):
    in_specs = (
        P("layer", "gx", "gy", None, None),
        P("layer", "gx", "gy", None, None),
        P("layer", "gx", "gy", None, None),
        P("layer", "gx", "gy", None),
    )
    out_specs = (P("layer", "gx", "gy", None, None), P("layer", "gx", "gy", None, None))
    return jax.shard_map(body, mesh=mesh, in_specs=in_specs, out_specs=out_specs, check_vma=False)
```

```python
import math

import jax
import jax.numpy as jnp
import numpy as np
from jax import lax
from jax.experimental import pallas as pl
from jax.experimental.pallas import tpu as pltpu
from jax.sharding import PartitionSpec as P

MESH = pl.DeviceIdType.MESH
PATCH_X = 14
PATCH_Y = 4

v_pi = -2.7
v_sigma = 0.48
decay_len = 0.319
layer_gap = 3.35 / 1.42
cut_radius = 3.5
hop_scale = 12.0
twist_angle = 1.05 * math.pi / 180.0
root_three = math.sqrt(3.0)
cell_w = 4.0 * root_three
cell_h = 24.0
reach = 0.15

COLS = 8
RIM = 2
WIDE = COLS + 2 * RIM
STEPS = 5
ROWS = 32
GROUP = 4
atom_x = (0.0, root_three / 2.0, root_three / 2.0, 0.0)
atom_y = (0.0, 0.5, 1.5, 2.0)


def near_offsets():
    cos_t, sin_t = math.cos(twist_angle), math.sin(twist_angle)
    cells = []
    for s in range(4):
        col, row = np.meshgrid(np.arange(4 * PATCH_X), np.arange(8 * PATCH_Y), indexing="ij")
        x = (col - 2 * PATCH_X) * root_three + atom_x[s]
        y = (row - 4 * PATCH_Y) * 3.0 + atom_y[s]
        cells.append(np.stack([x.ravel(), y.ravel()], -1))
    places = np.concatenate(cells)
    turn = np.array([[cos_t - 1.0, -sin_t], [sin_t, cos_t - 1.0]])
    drift = places @ turn.T
    drift = np.concatenate([drift, -drift])
    slack = 2.0 * reach + 1e-3
    flat = math.sqrt(cut_radius**2 - layer_gap**2)
    plane, inter = [], []
    for step in range(-STEPS - 2, STEPS + 3):
        for col in range(-RIM - 2, RIM + 3):
            hit_plane = hit_inter = False
            for s in range(4):
                t = (s + step) % 4
                x = atom_x[s] - atom_x[t] - col * root_three
                y = atom_y[s] - atom_y[t] - 3.0 * ((s + step) // 4)
                hit_plane |= math.hypot(x, y) - slack * math.sqrt(2.0) < cut_radius
                gap = np.maximum(np.abs(np.array([x, y]) + drift) - slack, 0.0)
                hit_inter |= bool((np.hypot(gap[:, 0], gap[:, 1]) < flat).any())
            if hit_plane and (col, step) != (0, 0):
                plane.append((col, step))
            if hit_inter:
                inter.append((col, step))
    assert max(abs(c) for c, _ in plane + inter) <= RIM
    assert max(abs(s) for _, s in plane + inter) <= STEPS
    return plane, inter


PLANE, INTER = near_offsets()
TILE = (1, 0, 0)
SIDES = [(a, b, 0) for a in (0, 1) for b in (-1, 1)]
ENDS = [(a, 0, c) for a in (0, 1) for c in (-1, 1)]
CORNERS = [(a, b, c) for a in (0, 1) for b in (-1, 1) for c in (-1, 1)]
LEFT = [(a, -1, 0) for a in (0, 1)]
RIGHT = [(a, 1, 0) for a in (0, 1)]
PEERS = [TILE] + ENDS
MESSAGES = 41
VMEM_LIMIT = 40 * 1024 * 1024


def peer(step):
    sizes = [lax.axis_size(a) for a in ("layer", "gx", "gy")]
    return tuple(
        lax.rem(lax.axis_index(a) + s + n, n) for a, s, n in zip(("layer", "gx", "gy"), step, sizes)
    )


def pick(index, table):
    value = jnp.full(index.shape, table[3], jnp.float32)
    for s in range(3):
        value = jnp.where(index == s, jnp.float32(table[s]), value)
    return value


def regroup(parts, lane):
    group = lane // 32
    results = []
    for a in range(4):
        value = parts[a]
        for b in range(4):
            if b != a:
                value = jnp.where(group == b, pltpu.roll(parts[b], (32 * (b - a)) % 128, 1), value)
        results.append(value)
    return results


def kernel(
    prev_hbm, cur_hbm, disp_hbm, pot_hbm, result,
    prev_in, cur_in, disp_in, pot_in, pot_t, prev_t, second_t, wide, wide2,
    end_out, end_in, end_out2, end_in2, spot_in,
    rims, spot, spot_rim, near_plane, near_inter, own_spot, hop_plane, hop_inter,
    load_sem, send_sem, recv_sem, corner_sem, left_sem,
):
    barrier = pltpu.get_barrier_semaphore()
    for step in PEERS + LEFT:
        pl.semaphore_signal(barrier, inc=1, device_id=peer(step), device_id_type=MESH)
    loads = [
        pltpu.make_async_copy(src, dst, load_sem.at[i])
        for i, (src, dst) in enumerate(
            ((disp_hbm, disp_in), (cur_hbm, cur_in), (prev_hbm, prev_in), (pot_hbm, pot_in))
        )
    ]
    for load in loads:
        load.start()
    lane = lax.broadcasted_iota(jnp.int32, (8, 128), 1)
    zero = jnp.zeros((8, 128), jnp.float32)
    sent = []

    def send(source, target, step):
        n = len(sent)
        assert n < MESSAGES
        copy = pltpu.make_async_remote_copy(
            src_ref=source,
            dst_ref=target,
            send_sem=send_sem.at[n],
            recv_sem=recv_sem.at[n],
            device_id=peer(step),
            device_id_type=MESH,
        )
        copy.start()
        sent.append(copy)
        return copy

    def send_side(buffer, layer, gx):
        source, target = (COLS, 0) if gx > 0 else (RIM, RIM + COLS)
        return send(
            buffer.at[0, pl.ds(source, RIM)], buffer.at[layer, pl.ds(target, RIM)], (layer, gx, 0)
        )

    def send_tile(buffer, first, count):
        where = pl.ds(RIM + first, count)
        return send(buffer.at[0, where], buffer.at[1, where], TILE)

    def send_end(source, target, step):
        layer, gx, gy = step
        end = 0 if gy > 0 else 1
        return send(source.at[end], target.at[1 - gx, layer, end], step)

    def to_columns(source, target, first):
        for x in range(2):
            for g in range(ROWS // 8):
                parts = [source[0, x, y, 8 * g : 8 * g + 8, :] for y in range(4)]
                for i, value in enumerate(regroup(parts, lane)):
                    target[first + 4 * x + i, 8 * g : 8 * g + 8, :] = value

    def pack_ends(source, targets, columns, ends=None):
        low, high = ends or (zero, zero)
        for k in range(4 * columns.start, 4 * columns.stop):
            value = source[0, RIM + k // 4, 8 * (k % 4) : 8 * (k % 4) + 8, :]
            value = pltpu.roll(value, (4 * k + 4) % 128, 1)
            low = jnp.where(lane // 4 == k, value, low)
            high = jnp.where(lane // 4 == (k + 1) % 32, value, high)
        targets[0, 0:8, :] = low
        targets[1, 0:8, :] = high
        return low, high

    loads[0].wait()
    for x in range(2):
        for i, value in enumerate(regroup([disp_in[0, x, y] for y in range(4)], lane[:2])):
            for axis in range(2):
                spot_in[1, 0, axis, 4 * x + i : 4 * x + i + 1, :] = value[axis : axis + 1]
    for end in range(2):
        moved = pltpu.roll(spot_in[1, 0, 1], 4 if end else 124, 1)
        keep = lane < 4 if end else lane >= 124
        end_out[end, 8:16, :] = jnp.where(keep, spot_in[1, 0, 0], moved)
    loads[1].wait()
    to_columns(cur_in, wide.at[0], RIM)
    pack_ends(wide, end_out, range(COLS))

    def tell(sem, steps):
        for step in steps:
            pl.semaphore_signal(sem, inc=1, device_id=peer(step), device_id_type=MESH)

    def send_spots(steps):
        return [send(spot_in.at[1, 0], spot_in.at[1 - gx, layer], (layer, gx, gy)) for layer, gx, gy in steps]

    pl.semaphore_wait(barrier, len(PEERS + RIGHT))
    tell(left_sem, RIGHT)
    tell(corner_sem.at[0], [(0, 0, -1), (0, 0, 1)])
    near_right = [send_end(end_out, end_in, step) for step in ENDS]
    near_right += send_spots([TILE])
    near_left = send_spots(RIGHT)
    right_tile = send_tile(wide, 2, COLS - 2)
    left_rim = [send_side(wide, layer, 1) for layer in (1, 0)]
    left_tile = send_tile(wide, 0, 2)
    pl.semaphore_wait(corner_sem.at[0], 2)
    near_left += [send_end(end_out, end_in, step) for step in CORNERS if step[1] > 0]
    pl.semaphore_wait(left_sem, 2)
    tell(corner_sem.at[1], [(0, 0, -1), (0, 0, 1)])
    near_right += send_spots(LEFT)
    right_rim = [send_side(wide, layer, -1) for layer in (1, 0)]
    pl.semaphore_wait(corner_sem.at[1], 2)
    near_right += [send_end(end_out, end_in, step) for step in CORNERS if step[1] < 0]

    loads[2].wait()
    to_columns(prev_in, prev_t, 0)
    loads[3].wait()
    for x in range(2):
        for i, value in enumerate(regroup([pot_in[0, x, y : y + 1] for y in range(4)], lane[:1])):
            pot_t[4 * x + i : 4 * x + i + 1, :] = value

    def rim_of(col):
        side = 0 if col < RIM else (1 if col < RIM + COLS else 2)
        return side, (col + COLS - RIM) % COLS

    def end_levels(low, high, k):
        picked = jnp.where(((lane + (124 - 4 * k)) & 127) < 64, high, low)
        return pltpu.roll(picked, 124 - 4 * k, 1)

    def with_rim(sides):
        return jnp.concatenate([sides[0][COLS - RIM :], sides[1], sides[2][:RIM], zero[:4]], axis=0)

    def end_spot(side, layer, axis):
        low, high = end_in[side, layer, 0, 8:16, :], end_in[side, layer, 1, 8:16, :]
        if axis:
            low, high = pltpu.roll(low, 4, 1), pltpu.roll(high, 124, 1)
        return jnp.where(lane < 64, high, low)

    layer_id = lax.axis_index("layer")
    cos_t, sin_t = math.cos(twist_angle), math.sin(twist_angle)
    upper = layer_id == 1
    cos_own = jnp.where(upper, jnp.float32(cos_t), jnp.float32(1.0))
    sin_own = jnp.where(upper, jnp.float32(sin_t), jnp.float32(0.0))

    row16 = lax.broadcasted_iota(jnp.int32, (16, 128), 0)
    lane16 = lax.broadcasted_iota(jnp.int32, (16, 128), 1)
    atom = lane16 & 3
    block = (lax.axis_index("gx") * 2 + (row16 + RIM) // 4 - 1 + 2 * lax.axis_size("gx")) % (
        2 * lax.axis_size("gx")
    )
    at_x = (
        ((row16 + RIM) & 3).astype(jnp.float32) * root_three
        + pick(atom, atom_x)
        - cell_w / 2.0
        + cell_w * ((block % PATCH_X).astype(jnp.float32) - (PATCH_X - 1) / 2.0)
    )
    at_y = (
        ((lane16 // 4) & 7).astype(jnp.float32) * 3.0
        + pick(atom, atom_y)
        - cell_h / 2.0
        + cell_h * ((lane16 // 32).astype(jnp.float32) - (PATCH_Y - 1) / 2.0)
    )
    turn_x = (cos_t - 1.0) * at_x - sin_t * at_y
    turn_y = sin_t * at_x + (cos_t - 1.0) * at_y
    own_on = jnp.where(upper, jnp.float32(1.0), jnp.float32(0.0))
    other_on = 1.0 - own_on

    def unturned(ref):
        return (
            cos_own * ref[0, 0] + sin_own * ref[0, 1],
            cos_own * ref[0, 1] - sin_own * ref[0, 0],
        )

    turns = (turn_x, turn_y)

    def joined(here, rim, step, lanes):
        if step > 0:
            return jnp.where(lanes < step, rim, here)
        if step < 0:
            return jnp.where(lanes >= 128 + step, rim, here)
        return here

    def rolled_by(value, step):
        return pltpu.roll(value, step % 128, 1) if step else value

    inner = slice(RIM, RIM + COLS)
    def find_spots(sides):
        blank = [zero] * 3
        for layer in range(2):
            for axis in range(2):
                here, rim = list(blank), list(blank)
                for side in sides:
                    here[side] = spot_in[side, layer, axis]
                    rim[side] = end_spot(side, layer, axis)
                spot[layer, axis] = with_rim(here)
                spot_rim[layer, axis] = with_rim(rim)
        plane_here, plane_rim = unturned(spot), unturned(spot_rim)
        for axis in range(2):
            near_plane[axis, 0] = plane_here[axis]
            near_plane[axis, 1] = plane_rim[axis]
            near_inter[axis, 0] = spot[1, axis] + other_on * turns[axis]
            near_inter[axis, 1] = spot_rim[1, axis] + other_on * turns[axis]
            own_spot[axis] = near_plane[axis, 0, inner, :]
            own_spot[2 + axis] = spot[0, axis, inner, :] + own_on * turns[axis][inner]

    def atom_heights(index):
        return (index >> 2).astype(jnp.float32) * 3.0 + pick(index & 3, atom_y)

    log2e = 1.0 / math.log(2.0)
    inverse_cut = 1.0 / (cut_radius * cut_radius)
    scale = 2.0 / hop_scale
    sigma_part = v_sigma * math.exp((layer_gap - 1.0) / decay_len)

    def parts(first, near, col, step):
        base_x = pick((lane - step + 8) & 3, atom_x) - pick(lane & 3, atom_x)
        base_y = atom_heights(lane - step + 8) - atom_heights(lane + 8)
        rows = slice(RIM + col, RIM + col + COLS)
        own = [rolled_by(own_spot[first + axis], step) for axis in range(2)]
        other = [joined(near[axis, 0, rows, :], near[axis, 1, rows, :], step, lane) for axis in range(2)]
        delta_x = (own[0] - other[0]) + (base_x - col * root_three)
        delta_y = (own[1] - other[1]) + base_y
        return delta_x * delta_x + delta_y * delta_y

    def envelope(dist_sq, inverse):
        spread = dist_sq * inverse
        fall = jnp.exp2(spread * (-log2e / decay_len) + log2e / decay_len)
        scaled = dist_sq * inverse_cut
        return fall * jnp.maximum(1.0 - scaled * scaled, 0.0)

    def find_hops():
        for n, (col, step) in enumerate(PLANE):
            dist_sq = parts(0, near_plane, col, step)
            hop_plane[n] = envelope(dist_sq, lax.rsqrt(dist_sq)) * (v_pi * scale)
        for n, (col, step) in enumerate(INTER):
            dist_sq = parts(2, near_inter, col, step) + layer_gap * layer_gap
            inverse = lax.rsqrt(dist_sq)
            cosine_sq = (inverse * inverse) * (layer_gap * layer_gap)
            mix = cosine_sq * ((sigma_part - v_pi) * scale) + v_pi * scale
            hop_inter[n] = envelope(dist_sq, inverse) * mix

    def unpack_ends(ends, columns):
        for layer in range(2):
            for col in columns:
                side, own = rim_of(col)
                for g in range(4):
                    low, high = ends[side, layer, 0, 0:8, :], ends[side, layer, 1, 0:8, :]
                    rims[layer, col, 8 * g : 8 * g + 8, :] = end_levels(low, high, own * 4 + g)

    def apply(buffer, minus, minus_first, target, target_first, first, count):
        def columns(group, carry):
            base = group * GROUP
            total = {}
            for d in range(GROUP):
                onsite = jnp.broadcast_to(pot_t[pl.ds(base + d, 1), :] * scale, (8, 128))
                for g in range(4):
                    rows = slice(8 * g, 8 * g + 8)
                    total[d, g] = (
                        onsite * buffer[0, base + d + RIM, rows, :] - minus[base + d + minus_first, rows, :]
                    )
            for step in range(-STEPS, STEPS + 1):
                part = {}
                for layer, (offsets, hops) in enumerate(((PLANE, hop_plane), (INTER, hop_inter))):
                    here = [(n, dcol) for n, (dcol, s) in enumerate(offsets) if s == step]
                    weight = {
                        (n, d): jnp.broadcast_to(hops[n, pl.ds(base + d, 1), :], (8, 128))
                        for n, _ in here
                        for d in range(GROUP)
                    }
                    for c in range(GROUP + 2 * RIM):
                        users = [(n, c - RIM - dcol) for n, dcol in here if 0 <= c - RIM - dcol < GROUP]
                        for g in range(4):
                            rows = slice(8 * g, 8 * g + 8)
                            near = buffer[layer, base + c, rows, :]
                            if step:
                                near = joined(near, rims[layer, base + c, rows, :], step, lane)
                            for n, d in users:
                                term = weight[n, d] * near
                                part[d, g] = part[d, g] + term if (d, g) in part else term
                for key, value in part.items():
                    total[key] = total[key] + rolled_by(value, -step)
            for (d, g), value in total.items():
                target[base + d + target_first, 8 * g : 8 * g + 8, :] = value
            return carry

        lax.fori_loop(first // GROUP, (first + count) // GROUP, columns, 0)

    def to_blocks(source, first, n):
        for x in range(2):
            for g in range(ROWS // 8):
                columns = [source[first + 4 * x + i, 8 * g : 8 * g + 8, :] for i in range(4)]
                for y, value in enumerate(regroup(columns, lane)):
                    result[n, 0, x, y, 8 * g : 8 * g + 8, :] = value

    half = COLS // 2
    right_wide, left_wide = range(half, WIDE), range(half)

    def arrive(copies):
        for copy in copies:
            copy.wait_recv()

    arrive(near_right)
    find_spots((1, 2))
    find_hops()
    unpack_ends(end_in, right_wide)
    arrive(right_rim + [right_tile])
    apply(wide, prev_t, 0, wide2.at[0], RIM, half, half)
    from_left = [send_side(wide2, layer, 1) for layer in (1, 0)]
    tile2 = [send_tile(wide2, half, half)]
    packed = pack_ends(wide2, end_out2.at[0], range(half, COLS))
    from_left += [send_end(end_out2.at[0], end_in2, step) for step in CORNERS if step[1] > 0]
    arrive(near_left)
    find_spots((0, 1, 2))
    find_hops()
    unpack_ends(end_in, left_wide)
    arrive(left_rim + [left_tile])
    apply(wide, prev_t, 0, wide2.at[0], RIM, 0, half)
    tile2.append(send_tile(wide2, 0, half))
    from_right = [send_side(wide2, layer, -1) for layer in (1, 0)]
    pack_ends(wide2, end_out2.at[1], range(half), packed)
    from_right += [
        send_end(end_out2.at[1], end_in2, step) for step in ENDS + CORNERS if step[1] <= 0
    ]
    to_blocks(wide2.at[0], RIM, 0)
    for copy in sent:
        copy.wait_send()
    arrive(tile2 + from_right)
    unpack_ends(end_in2, right_wide)
    apply(wide2, wide.at[0], RIM, second_t, 0, half, half)
    arrive(from_left)
    unpack_ends(end_in2, left_wide)
    apply(wide2, wide.at[0], RIM, second_t, 0, 0, half)
    to_blocks(second_t, 0, 1)


def finish(result, first_ref, second_ref, sem):
    copies = [
        pltpu.make_async_copy(result.at[n], target, sem.at[n])
        for n, target in enumerate((first_ref, second_ref))
    ]
    for copy in copies:
        copy.start()
    for copy in copies:
        copy.wait()


def body(prev_vec, cur_vec, displace, potential):
    f32 = jnp.float32
    near = pltpu.VMEM((2, 2, 16, 128), f32)
    hbm, vmem = pl.BlockSpec(memory_space=pltpu.HBM), pl.BlockSpec(memory_space=pltpu.VMEM)
    result = pl.pallas_call(
        kernel,
        out_shape=pltpu.VMEM((2,) + cur_vec.shape, f32),
        in_specs=[hbm] * 4,
        out_specs=pl.BlockSpec(memory_space=pltpu.VMEM),
        scratch_shapes=[
            pltpu.VMEM(prev_vec.shape, f32),
            pltpu.VMEM(cur_vec.shape, f32),
            pltpu.VMEM(displace.shape, f32),
            pltpu.VMEM(potential.shape, f32),
            pltpu.VMEM((COLS, 128), f32),
            pltpu.VMEM((COLS, ROWS, 128), f32),
            pltpu.VMEM((COLS, ROWS, 128), f32),
            pltpu.VMEM((2, WIDE, ROWS, 128), f32),
            pltpu.VMEM((2, WIDE, ROWS, 128), f32),
            pltpu.VMEM((2, 16, 128), f32),
            pltpu.VMEM((3, 2, 2, 16, 128), f32),
            pltpu.VMEM((2, 2, 8, 128), f32),
            pltpu.VMEM((3, 2, 2, 8, 128), f32),
            pltpu.VMEM((3, 2, 2, COLS, 128), f32),
            pltpu.VMEM((2, WIDE, ROWS, 128), f32),
            near,
            near,
            near,
            near,
            pltpu.VMEM((4, COLS, 128), f32),
            pltpu.VMEM((len(PLANE), COLS, 128), f32),
            pltpu.VMEM((len(INTER), COLS, 128), f32),
            pltpu.SemaphoreType.DMA((4,)),
            pltpu.SemaphoreType.DMA((MESSAGES,)),
            pltpu.SemaphoreType.DMA((MESSAGES,)),
            pltpu.SemaphoreType.REGULAR((2,)),
            pltpu.SemaphoreType.REGULAR,
        ],
        compiler_params=pltpu.CompilerParams(
            collective_id=0, has_side_effects=True, vmem_limit_bytes=VMEM_LIMIT
        ),
        name="two_terms",
    )(*[pltpu.with_memory_space_constraint(x, pltpu.HBM) for x in (prev_vec, cur_vec, displace, potential)])
    return pl.pallas_call(
        finish,
        out_shape=(jax.ShapeDtypeStruct(cur_vec.shape, f32),) * 2,
        in_specs=[vmem],
        out_specs=(hbm, hbm),
        scratch_shapes=[
            pltpu.SemaphoreType.DMA((2,)),
        ],
        compiler_params=pltpu.CompilerParams(vmem_limit_bytes=VMEM_LIMIT),
        name="finish",
    )(result)


def solution(mesh):
    in_specs = (
        P("layer", "gx", "gy", None, None),
        P("layer", "gx", "gy", None, None),
        P("layer", "gx", "gy", None, None),
        P("layer", "gx", "gy", None),
    )
    out_specs = (P("layer", "gx", "gy", None, None), P("layer", "gx", "gy", None, None))
    return jax.shard_map(body, mesh=mesh, in_specs=in_specs, out_specs=out_specs, check_vma=False)
```
